32 devices in a mesh: angle: 8 (over y, x, core), frame: 4 (over z).
Axes of the slice: x: 2, y: 2, z: 4, core: 2. Of those that a mesh axis runs over, the one named last changes fastest.
Arguments:
- volume: float32 [32, 8192], P('frame', 'angle'), may hold values from -6 to 6
- measured: bfloat16 [8, 32, 12288], P(None, 'frame', 'angle'), may hold values from -6 to 6
- tiles: bfloat16 [8, 1024, 1536], replicated, may hold values from -0.0625 to 0.0625
- tile_index: int32 [8, 8], replicated, may hold values from 0 to 7, as said below
- warp_coef: bfloat16 [8, 3, 32, 8192], P(None, None, 'frame', 'angle'), may hold values from 0.099609375 to 0.59765625
- warp_offset: int32 [8, 32], P(None, 'frame'), may hold values from -2 to 0
- ray_weight: float32 [32, 12288], P('frame', 'angle'), may hold values from 0.5 to 2
- redundancy: float32 [12288], P('angle'), may hold values from 0.2 to 0.8
- conj_view: int32 [8, 2], P('angle'), may hold values from 0 to 1, as said below
- voxel_weight: float32 [32, 8192], P('frame', 'angle'), may hold values from 0.05 to 0.2
Outputs:
- volume_next: float32 [32, 8192], P('frame', 'angle')
- weighted: bfloat16 [8, 32, 12288], P(None, 'frame', 'angle')
The draws below stay inside these ranges and needn't reach their ends.
Inputs may be any that keep to these rules, and one draw needn't show every extreme that they name: `conj_view`: each row is a permutation of 0..1, and row b + 4 is the inverse permutation of row b for b < 4. `tile_index`: every row is a permutation of 0..7.
All inputs are finite; a program needn't handle non-finite values.
Results may differ from the reference program's by a relative error of at most 0.0034.
Values may be sent and summed in bfloat16 or wider, within the bound.
A program may use at most 256 MiB of HBM per device.

```python
import math
import jax
import jax.numpy as jnp
from jax import lax

F = 8
VS = 1024
VB = 2
UW = 768
TAPS = 3
HALO = 2
Z = 32
BLOCKS = 8
TB = 8
V = 8192
P_SIZE = 1536
RAYS = 12288


def draw_conj_view(key, part):
    half_count = BLOCKS // 2
    keys = jax.random.split(key, half_count)
    onward = jax.vmap(lambda one_key: jax.random.permutation(one_key, VB))(keys).astype(jnp.int32)
    inverse = jnp.argsort(onward, axis=1).astype(jnp.int32)
    return jnp.concatenate([onward, inverse], axis=0)


def draw_tile_index(key, part):
    row_keys = jax.random.split(jax.random.fold_in(key, 7), BLOCKS)
    rows = jax.vmap(lambda one_key: jax.random.permutation(one_key, TB))(row_keys)
    return rows.astype(jnp.int32)


def place_ends(entries, own_key, smallest, high):
    shape = entries.shape
    index_at = [jax.random.randint(jax.random.fold_in(own_key, axis), (), 0, shape[axis]) for axis in range(len(shape))]
    entries = entries.at[tuple(index_at)].set(smallest)
    longest = shape.index(max(shape))
    index_at[longest] = (index_at[longest] + 1) % shape[longest]
    return entries.at[tuple(index_at)].set(high)


def block_levels(stream_key, extent, cuts, smallest, largest):
    gain = 1.0
    for dim, parts in cuts:
        steps = jax.random.uniform(jax.random.fold_in(jax.random.fold_in(stream_key, 6), dim), (parts,), jnp.float32, smallest / len(cuts), largest / len(cuts))
        gain = gain * jnp.repeat(jnp.exp(steps), extent[dim] // parts).reshape((-1,) + (1,) * (len(extent) - 1 - dim))
    return gain


def normal_values(rng, shape, deviation, limit, cuts=(), held_as=jnp.bfloat16):
    result = jax.random.normal(rng, shape, jnp.float32) * deviation
    if len(cuts) > 0:
        result = block_levels(rng, shape, cuts, -0.22, 0.18) * result
    return jnp.clip(result, min=-limit, max=limit).astype(held_as)


def setup_inputs(seed: int = 0) -> dict:
    key_list = jax.random.split(jax.random.key(seed), 11)
    return {
        "volume": normal_values(key_list[0], (Z, V), 1.0, 6.0, ((0, 4), (1, 8)), jnp.float32),
        "measured": normal_values(key_list[1], (F, Z, RAYS), 1.0, 6.0, ((1, 4), (2, 8))),
        "tiles": normal_values(key_list[2], (TB, VS, P_SIZE), V ** -0.5, 0.0625),
        "tile_index": draw_tile_index(jax.random.fold_in(key_list[10], 71), 0),
        "warp_coef": jnp.clip(0.099609375 + 0.49804688 * jax.random.uniform(key_list[4], (F, TAPS, Z, V), jnp.float32) ** block_levels(key_list[4], (F, TAPS, Z, V), ((2, 4), (3, 8)), -0.2, 0.2), 0.099609375, 0.59765625).astype(jnp.bfloat16),
        "warp_offset": place_ends(jax.random.randint(key_list[5], (F, Z), 0 - HALO, 1), jax.random.fold_in(key_list[5], 1), 0 - HALO, 0).astype(jnp.int32),
        "ray_weight": jnp.clip(jnp.exp(math.log(2.0) - 1.3862944 * jax.random.uniform(key_list[6], (Z, RAYS), jnp.float32) ** block_levels(key_list[6], (Z, RAYS), ((0, 4), (1, 8)), -0.2, 0.2)), 0.5, 2.0),
        "redundancy": jnp.clip(0.2 + 0.6 * jax.random.uniform(key_list[7], (RAYS,), jnp.float32) ** block_levels(key_list[7], (RAYS,), ((0, 8),), -0.2, 0.2), 0.2, 0.8),
        "conj_view": draw_conj_view(jax.random.fold_in(key_list[10], 71), 0),
        "voxel_weight": jnp.clip(jnp.exp(math.log(0.2) - 1.3862944 * jax.random.uniform(key_list[9], (Z, V), jnp.float32) ** block_levels(key_list[9], (Z, V), ((0, 4), (1, 8)), -0.2, 0.2)), 0.05, 0.2),
    }


def warp_weights(offsets, coefs, distance):
    weights = jnp.zeros(coefs[:, 0].shape, jnp.float32)
    for tap_index in range(coefs.shape[1]):
        selected = (offsets + tap_index == distance).astype(jnp.float32)[:, :, None]
        weights = weights + selected * coefs[:, tap_index].astype(jnp.float32)
    return weights


def reference(volume, measured, tiles, tile_index, warp_coef, warp_offset, ray_weight, redundancy, conj_view, voxel_weight):
    padded = jnp.pad(volume, ((HALO, HALO), (0, 0)))
    warped = jnp.zeros((F, Z, V), jnp.float32)
    for distance in range(-HALO, HALO + 1):
        source_rows = padded[HALO + distance:HALO + distance + Z]
        warped = warped + warp_weights(warp_offset, warp_coef, distance) * source_rows[None]
    stacked_rows = warped.astype(jnp.bfloat16).reshape(F * Z, V)

    def project_block(block):
        def add_sector(sector_no, running):
            part = lax.dynamic_slice_in_dim(stacked_rows, sector_no * VS, VS, 1)
            footprint = tiles[tile_index[block, sector_no]]
            return running + jnp.dot(part, footprint, preferred_element_type=jnp.float32)
        return lax.fori_loop(0, BLOCKS, add_sector, jnp.zeros((F * Z, P_SIZE), jnp.float32))

    projected = lax.map(project_block, jnp.arange(BLOCKS, dtype=jnp.int32))
    projected = projected.reshape(BLOCKS, F, Z, P_SIZE).transpose(1, 2, 0, 3).reshape(F, Z, RAYS)
    residual = measured.astype(jnp.float32) - projected
    block_view = residual.reshape(F, Z, BLOCKS, VB, UW)
    partner = jnp.roll(block_view, -(BLOCKS // 2), axis=2)
    picks = jnp.broadcast_to(conj_view[None, None, :, :, None], (F, Z, BLOCKS, VB, UW))
    mirrored = jnp.take_along_axis(partner, picks, axis=3)[..., ::-1].reshape(F, Z, RAYS)
    weighted = ((redundancy * residual + (1.0 - redundancy) * mirrored) * ray_weight[None]).astype(jnp.bfloat16)
    ray_rows = weighted.reshape(F * Z, RAYS)

    def back_sector(sector_no):
        def add_block(block, running):
            part = lax.dynamic_slice_in_dim(ray_rows, block * P_SIZE, P_SIZE, 1)
            footprint = tiles[tile_index[block, sector_no]]
            return running + lax.dot_general(part, footprint, (((1,), (1,)), ((), ())), preferred_element_type=jnp.float32)
        return lax.fori_loop(0, BLOCKS, add_block, jnp.zeros((F * Z, VS), jnp.float32))

    images = lax.map(back_sector, jnp.arange(BLOCKS, dtype=jnp.int32))
    images = images.transpose(1, 0, 2).reshape(F, Z, V)
    gathered = jnp.zeros((Z, V), jnp.float32)
    for distance in range(-HALO, HALO + 1):
        terms = jnp.sum(warp_weights(warp_offset, warp_coef, distance) * images, axis=0)
        padded_terms = jnp.pad(terms, ((HALO, HALO), (0, 0)))
        gathered = gathered + padded_terms[HALO - distance:HALO - distance + Z]
    return volume + voxel_weight * gathered, weighted
```

```python
import functools

import jax
import jax.numpy as jnp
from jax import lax
from jax.experimental import pallas as pl
from jax.experimental.pallas import tpu as pltpu
from jax.sharding import PartitionSpec as P

VB = 2
HALO = 2
TAPS = 3
MESH = pl.DeviceIdType.MESH
F32 = jnp.float32
BF16 = jnp.bfloat16


def kernel(
    blocks,
    slabs,
    frames,
    rows,
    volume,
    measured,
    tiles_hbm,
    tile_index,
    coefs,
    offsets,
    ray_weight,
    redundancy,
    conj_view,
    voxel_weight,
    next_ref,
    weighted_ref,
    tiles,
    gathered,
    proj,
    part_measured,
    part_weight,
    part_red,
    part_weighted,
    vol_out,
    vol_in,
    adj_out,
    adj_in,
    sib_out,
    sib_in,
    far_out,
    far_in,
    tile_sem,
    ag_send,
    ag_recv,
    fw_send,
    fw_recv,
    pt_send,
    pt_recv,
    hv_send,
    hv_recv,
    ha_send,
    ha_recv,
    sb_send,
    sb_recv,
    fr_send,
    fr_recv,
):
    me = lax.axis_index("angle")
    slab = lax.axis_index("frame")
    half = blocks // 2
    chips = blocks // 2
    core = lax.rem(me, 2)
    chip = me // 2
    sibling = me + 1 - 2 * core
    partner = lax.rem(me + half, blocks)
    count = tiles.shape[0]
    stacked = frames * rows
    sector = volume.shape[1]
    rays = measured.shape[1]
    view = rays // VB
    has_low = slab > 0
    has_high = slab < slabs - 1

    def remote(src, dst, send, recv, angle, frame=slab):
        return pltpu.make_async_remote_copy(
            src_ref=src,
            dst_ref=dst,
            send_sem=send,
            recv_sem=recv,
            device_id=(angle, frame),
            device_id_type=MESH,
        )

    def tile_copy(t):
        return pltpu.make_async_copy(tiles_hbm.at[t], tiles.at[t], tile_sem.at[t])

    for t in range(count):
        tile_copy(t).start()

    barrier = pltpu.get_barrier_semaphore()
    pl.semaphore_signal(barrier, inc=1, device_id=(sibling, slab), device_id_type=MESH)
    for d in range(1, chips):
        other = lax.rem(chip + d, chips) * 2 + core
        pl.semaphore_signal(barrier, inc=1, device_id=(other, slab), device_id_type=MESH)

    @pl.when(has_low)
    def _():
        pl.semaphore_signal(barrier, inc=1, device_id=(me, slab - 1), device_id_type=MESH)

    @pl.when(has_high)
    def _():
        pl.semaphore_signal(barrier, inc=1, device_id=(me, slab + 1), device_id_type=MESH)

    vol = volume[...]
    vol_out[0] = vol[:HALO]
    vol_out[1] = vol[rows - HALO :]

    peers = chips + has_low.astype(jnp.int32) + has_high.astype(jnp.int32)
    pl.semaphore_wait(barrier, peers)

    def halo(out, into, send, recv, side):
        return remote(
            out.at[side], into.at[1 - side], send.at[side], recv.at[1 - side], me, slab + 2 * side - 1
        )

    def exchange(out, into, send, recv):
        @pl.when(has_low)
        def _():
            halo(out, into, send, recv, 0).start()

        @pl.when(has_high)
        def _():
            halo(out, into, send, recv, 1).start()

    def exchange_wait(out, into, send, recv):
        @pl.when(has_low)
        def _():
            halo(out, into, send, recv, 0).wait_send()
            halo(out, into, send, recv, 1).wait_recv()

        @pl.when(has_high)
        def _():
            halo(out, into, send, recv, 1).wait_send()
            halo(out, into, send, recv, 0).wait_recv()

        @pl.when(slab == 0)
        def _():
            into[0] = jnp.zeros_like(into[0])

        @pl.when(slab == slabs - 1)
        def _():
            into[1] = jnp.zeros_like(into[1])

    exchange(vol_out, vol_in, hv_send, hv_recv)

    exchange_wait(vol_out, vol_in, hv_send, hv_recv)
    off = offsets[...].astype(F32)
    lane = lax.broadcasted_iota(jnp.int32, (rows, rows), 1)
    diagonal = lane == lax.broadcasted_iota(jnp.int32, (rows, rows), 0)

    def offset_column(f):
        spread = jnp.broadcast_to(off[f : f + 1, :], (rows, rows))
        return jnp.sum(jnp.where(diagonal, spread, 0.0), axis=1, keepdims=True)

    columns = [offset_column(f) for f in range(frames)]
    extended = jnp.concatenate([vol_in[0], vol, vol_in[1]], axis=0)
    sources = [extended[m : m + rows] for m in range(2 * HALO + 1)]
    group = 2 * TAPS * rows
    for p in range(frames // 2):
        taps = coefs[p * group : (p + 1) * group, :].astype(F32)
        pair = []
        for i in range(2):
            column = columns[2 * p + i]
            low = column == -2.0
            mid = column == -1.0
            total = None
            for k in range(TAPS):
                start = (i * TAPS + k) * rows
                chosen = jnp.where(
                    low, sources[k], jnp.where(mid, sources[k + 1], sources[k + 2])
                )
                term = taps[start : start + rows] * chosen
                total = term if total is None else total + term
            pair.append(total)
        gathered[me, 2 * p * rows : 2 * (p + 1) * rows, :] = jnp.concatenate(pair, axis=0).astype(
            BF16
        )

    def to_chip(d):
        target = lax.rem(chip + d, chips) * 2 + core
        return remote(gathered.at[me], gathered.at[me], ag_send.at[d], ag_recv.at[d], target)

    def from_chip(d):
        return lax.rem(chip + chips - d, chips) * 2 + core

    def to_sibling(d):
        source = from_chip(d)
        return remote(
            gathered.at[source], gathered.at[source], fw_send.at[d], fw_recv.at[d], sibling
        )

    order = sorted(range(1, chips), key=lambda d: (d != chips // 2, d))
    for d in order:
        to_chip(d).start()
    to_sibling(0).start()
    partner_copies = [
        remote(measured, part_measured, pt_send.at[0], pt_recv.at[0], partner),
        remote(ray_weight, part_weight, pt_send.at[1], pt_recv.at[1], partner),
        remote(redundancy, part_red, pt_send.at[2], pt_recv.at[2], partner),
    ]
    for copy in partner_copies:
        copy.start()
    for d in order:
        to_chip(d).wait_recv()
        to_sibling(d).start()
    for d in range(chips):
        to_sibling(d).wait_recv()

    def project(t, carry):
        tile_copy(t).wait()
        own_sector = jnp.int32(0)
        part_sector = jnp.int32(0)
        for s in range(blocks):
            own_sector = jnp.where(tile_index[me, s] == t, s, own_sector)
            part_sector = jnp.where(tile_index[partner, s] == t, s, part_sector)
        left = jnp.concatenate([gathered[own_sector], gathered[part_sector]], axis=0)
        for n in range(VB):
            span = slice(n * view, (n + 1) * view)
            proj[:, span] += jnp.dot(left, tiles[t, :, span], preferred_element_type=F32)
        return carry

    proj[...] = jnp.zeros_like(proj)
    lax.fori_loop(0, count, project, 0)

    for copy in partner_copies:
        copy.wait_recv()

    wide = 256
    flip = lax.broadcasted_iota(jnp.int32, (wide, wide), 0) + lax.broadcasted_iota(
        jnp.int32, (wide, wide), 1
    )
    flip = jnp.where(flip == wide - 1, 1.0, 0.0).astype(BF16)
    swap = conj_view[0, 0] == 1
    residuals = [
        measured[...].astype(F32) - proj[:stacked, :],
        part_measured[...].astype(F32) - proj[stacked:, :],
    ]
    mirrors = []
    for value in residuals:
        high = value.astype(BF16)
        rest = (value - high.astype(F32)).astype(BF16)
        pieces = []
        for w in range(VB):
            for u in range(view // wide):
                start = w * view + view - (u + 1) * wide
                pieces.append(
                    jnp.dot(high[:, start : start + wide], flip, preferred_element_type=F32)
                    + jnp.dot(rest[:, start : start + wide], flip, preferred_element_type=F32)
                )
        each = view // wide
        first = jnp.concatenate(pieces[:each], axis=1)
        second = jnp.concatenate(pieces[each:], axis=1)
        mirrors.append(
            jnp.concatenate(
                [jnp.where(swap, second, first), jnp.where(swap, first, second)], axis=1
            )
        )

    def combine(residual, mirrored, red, weight):
        value = red * residual + (1.0 - red) * mirrored
        return (value * jnp.concatenate([weight] * frames, axis=0)).astype(BF16)

    weighted_ref[...] = combine(residuals[0], mirrors[1], redundancy[...], ray_weight[...])
    part_weighted[...] = combine(residuals[1], mirrors[0], part_red[...], part_weight[...])

    def partial(s):
        contract = (((1,), (1,)), ((), ()))
        own = lax.dot_general(
            weighted_ref[...], tiles[tile_index[me, s]], contract, preferred_element_type=F32
        )
        other = lax.dot_general(
            part_weighted[...], tiles[tile_index[partner, s]], contract, preferred_element_type=F32
        )
        return own + other

    ring = half // 2
    side = me // half
    place = lax.rem(me, half) // 2

    def sector_at(d, c):
        return side * half + lax.rem(place + d, ring) * 2 + c

    def sib_copy(d):
        return remote(sib_out.at[d], sib_in.at[d], sb_send.at[d], sb_recv.at[d], sibling)

    def far_copy(d):
        return remote(far_out.at[d], far_in.at[d], fr_send.at[d], fr_recv.at[d], sector_at(d, core))

    for d in range(1, ring):
        sib_out[d] = partial(sector_at(d, 1 - core)).astype(BF16)
        sib_copy(d).start()
    for d in range(1, ring):
        value = partial(sector_at(d, core))
        sib_copy(d).wait_recv()
        far_out[d] = (value + sib_in[d].astype(F32)).astype(BF16)
        far_copy(d).start()
    sib_out[0] = partial(sector_at(0, 1 - core)).astype(BF16)
    sib_copy(0).start()
    image = partial(me)
    for d in range(1, ring):
        far_copy(d).wait_recv()
        image = image + far_in[d].astype(F32)
    sib_copy(0).wait_recv()
    image = image + sib_in[0].astype(F32)

    spread = [jnp.zeros((rows, sector), F32) for _ in range(2 * HALO + 1)]
    for p in range(frames // 2):
        taps = coefs[p * group : (p + 1) * group, :].astype(F32)
        for i in range(2):
            f = 2 * p + i
            column = columns[f]
            slices = image[f * rows : (f + 1) * rows]
            for k in range(TAPS):
                start = (i * TAPS + k) * rows
                term = taps[start : start + rows] * slices
                for j in range(HALO + 1):
                    spread[k + j] = spread[k + j] + jnp.where(
                        column == float(j - HALO), term, 0.0
                    )
    empty = jnp.zeros((HALO, sector), F32)
    total = None
    for m in range(2 * HALO + 1):
        parts = [jnp.zeros((m, sector), F32)] if m else []
        parts.append(spread[m])
        if m < 2 * HALO:
            parts.append(jnp.zeros((2 * HALO - m, sector), F32))
        padded = jnp.concatenate(parts, axis=0)
        total = padded if total is None else total + padded
    adj_out[0] = total[:HALO]
    adj_out[1] = total[rows + HALO :]
    exchange(adj_out, adj_in, ha_send, ha_recv)
    for d in order:
        to_chip(d).wait_send()
    for d in range(chips):
        to_sibling(d).wait_send()
    for copy in partner_copies:
        copy.wait_send()
    for d in range(ring):
        sib_copy(d).wait_send()
    for d in range(1, ring):
        far_copy(d).wait_send()
    exchange_wait(adj_out, adj_in, ha_send, ha_recv)
    middle = jnp.zeros((rows - 2 * HALO, sector), F32)
    edges = jnp.concatenate([adj_in[0], middle, adj_in[1]], axis=0)
    adjoint = total[HALO : rows + HALO] + edges
    next_ref[...] = vol + voxel_weight[...] * adjoint


def body(
    volume,
    measured,
    tiles,
    tile_index,
    warp_coef,
    warp_offset,
    ray_weight,
    redundancy,
    conj_view,
    voxel_weight,
):
    frames, rows, rays = measured.shape
    sector = volume.shape[1]
    blocks = lax.axis_size("angle")
    slabs = lax.axis_size("frame")
    stacked = frames * rows
    ring = blocks // 4
    vmem = pl.BlockSpec(memory_space=pltpu.VMEM)
    smem = pl.BlockSpec(memory_space=pltpu.SMEM)
    dma = pltpu.SemaphoreType.DMA
    flops = 8 * stacked * blocks * sector * rays
    volume_next, weighted = pl.pallas_call(
        functools.partial(kernel, blocks, slabs, frames, rows),
        out_shape=(
            jax.ShapeDtypeStruct(volume.shape, F32),
            jax.ShapeDtypeStruct((stacked, rays), BF16),
        ),
        in_specs=[
            vmem,
            vmem,
            pl.BlockSpec(memory_space=pl.ANY),
            smem,
            vmem,
            vmem,
            vmem,
            vmem,
            smem,
            vmem,
        ],
        out_specs=(vmem, vmem),
        scratch_shapes=[
            pltpu.VMEM(tiles.shape, BF16),
            pltpu.VMEM((blocks, stacked, sector), BF16),
            pltpu.VMEM((2 * stacked, rays), F32),
            pltpu.VMEM((stacked, rays), BF16),
            pltpu.VMEM(ray_weight.shape, F32),
            pltpu.VMEM((1, rays), F32),
            pltpu.VMEM((stacked, rays), BF16),
            pltpu.VMEM((2, HALO, sector), F32),
            pltpu.VMEM((2, HALO, sector), F32),
            pltpu.VMEM((2, HALO, sector), F32),
            pltpu.VMEM((2, HALO, sector), F32),
            pltpu.VMEM((ring, stacked, sector), BF16),
            pltpu.VMEM((ring, stacked, sector), BF16),
            pltpu.VMEM((ring, stacked, sector), BF16),
            pltpu.VMEM((ring, stacked, sector), BF16),
            dma((tiles.shape[0],)),
            dma((blocks // 2,)),
            dma((blocks // 2,)),
            dma((blocks // 2,)),
            dma((blocks // 2,)),
            dma((3,)),
            dma((3,)),
            dma((2,)),
            dma((2,)),
            dma((2,)),
            dma((2,)),
            dma((ring,)),
            dma((ring,)),
            dma((ring,)),
            dma((ring,)),
        ],
        cost_estimate=pl.CostEstimate(
            flops=flops, bytes_accessed=2 * tiles.size, transcendentals=0
        ),
        compiler_params=pltpu.CompilerParams(
            collective_id=0, has_side_effects=True, vmem_limit_bytes=62 * 1024 * 1024
        ),
    )(
        volume,
        measured.reshape(stacked, rays),
        tiles,
        tile_index,
        warp_coef.reshape(frames * TAPS * rows, sector),
        warp_offset,
        ray_weight,
        redundancy.reshape(1, rays),
        conj_view,
        voxel_weight,
    )
    return volume_next, weighted.reshape(frames, rows, rays)


def solution(mesh):
    placed = (
        P("frame", "angle"),
        P(None, "frame", "angle"),
        P(),
        P(),
        P(None, None, "frame", "angle"),
        P(None, "frame"),
        P("frame", "angle"),
        P("angle"),
        P("angle", None),
        P("frame", "angle"),
    )
    return jax.shard_map(
        body,
        mesh=mesh,
        in_specs=placed,
        out_specs=(P("frame", "angle"), P(None, "frame", "angle")),
        check_vma=False,
    )
```

```python
import functools

import jax
import jax.numpy as jnp
from jax import lax
from jax.experimental import pallas as pl
from jax.experimental.pallas import tpu as pltpu
from jax.sharding import PartitionSpec as P

VB = 2
HALO = 2
TAPS = 3
MESH = pl.DeviceIdType.MESH
F32 = jnp.float32
BF16 = jnp.bfloat16


def kernel(
    blocks,
    slabs,
    frames,
    rows,
    volume_hbm,
    measured_hbm,
    tiles_hbm,
    tile_index,
    coefs_hbm,
    offsets,
    weight_hbm,
    red_hbm,
    conj_view,
    voxel_hbm,
    next_hbm,
    weighted_hbm,
    volume,
    measured,
    coefs,
    ray_weight,
    redundancy,
    voxel_weight,
    next_ref,
    weighted_ref,
    tiles,
    gathered,
    proj,
    part_measured,
    part_weight,
    part_red,
    part_weighted,
    vol_out,
    vol_in,
    adj_out,
    adj_in,
    sib_out,
    sib_in,
    far_out,
    far_in,
    in_sem,
    out_sem,
    tile_sem,
    ag_send,
    ag_recv,
    fw_send,
    fw_recv,
    pt_send,
    pt_recv,
    hv_send,
    hv_recv,
    ha_send,
    ha_recv,
    sb_send,
    sb_recv,
    fr_send,
    fr_recv,
):
    me = lax.axis_index("angle")
    slab = lax.axis_index("frame")
    half = blocks // 2
    chips = blocks // 2
    core = lax.rem(me, 2)
    chip = me // 2
    sibling = me + 1 - 2 * core
    partner = lax.rem(me + half, blocks)
    count = tiles.shape[0]
    stacked = frames * rows
    sector = volume.shape[1]
    rays = measured.shape[1]
    view = rays // VB
    has_low = slab > 0
    has_high = slab < slabs - 1

    def remote(src, dst, send, recv, angle, frame=slab):
        return pltpu.make_async_remote_copy(
            src_ref=src,
            dst_ref=dst,
            send_sem=send,
            recv_sem=recv,
            device_id=(angle, frame),
            device_id_type=MESH,
        )

    def tile_copy(t):
        return pltpu.make_async_copy(tiles_hbm.at[t], tiles.at[t], tile_sem.at[t])

    barrier = pltpu.get_barrier_semaphore()
    pl.semaphore_signal(barrier, inc=1, device_id=(sibling, slab), device_id_type=MESH)
    for d in range(1, chips):
        other = lax.rem(chip + d, chips) * 2 + core
        pl.semaphore_signal(barrier, inc=1, device_id=(other, slab), device_id_type=MESH)

    @pl.when(has_low)
    def _():
        pl.semaphore_signal(barrier, inc=1, device_id=(me, slab - 1), device_id_type=MESH)

    @pl.when(has_high)
    def _():
        pl.semaphore_signal(barrier, inc=1, device_id=(me, slab + 1), device_id_type=MESH)

    local = [
        pltpu.make_async_copy(src, dst, in_sem.at[n])
        for n, (src, dst) in enumerate(
            (
                (volume_hbm, volume),
                (coefs_hbm, coefs),
                (measured_hbm, measured),
                (weight_hbm, ray_weight),
                (red_hbm, redundancy),
                (voxel_hbm, voxel_weight),
            )
        )
    ]
    for copy in local:
        copy.start()
    local[0].wait()
    vol = volume[...]
    vol_out[0] = vol[:HALO]
    vol_out[1] = vol[rows - HALO :]

    peers = chips + has_low.astype(jnp.int32) + has_high.astype(jnp.int32)
    pl.semaphore_wait(barrier, peers)

    def halo(out, into, send, recv, side):
        return remote(
            out.at[side], into.at[1 - side], send.at[side], recv.at[1 - side], me, slab + 2 * side - 1
        )

    def exchange(out, into, send, recv):
        @pl.when(has_low)
        def _():
            halo(out, into, send, recv, 0).start()

        @pl.when(has_high)
        def _():
            halo(out, into, send, recv, 1).start()

    def exchange_wait(out, into, send, recv):
        @pl.when(has_low)
        def _():
            halo(out, into, send, recv, 0).wait_send()
            halo(out, into, send, recv, 1).wait_recv()

        @pl.when(has_high)
        def _():
            halo(out, into, send, recv, 1).wait_send()
            halo(out, into, send, recv, 0).wait_recv()

        @pl.when(slab == 0)
        def _():
            into[0] = jnp.zeros_like(into[0])

        @pl.when(slab == slabs - 1)
        def _():
            into[1] = jnp.zeros_like(into[1])

    exchange(vol_out, vol_in, hv_send, hv_recv)

    off = offsets[...].astype(F32)
    lane = lax.broadcasted_iota(jnp.int32, (rows, rows), 1)
    diagonal = lane == lax.broadcasted_iota(jnp.int32, (rows, rows), 0)

    def offset_column(f):
        spread = jnp.broadcast_to(off[f : f + 1, :], (rows, rows))
        return jnp.sum(jnp.where(diagonal, spread, 0.0), axis=1, keepdims=True)

    columns = [offset_column(f) for f in range(frames)]
    group = 2 * TAPS * rows

    def warp(below, above):
        extended = jnp.concatenate([below, vol, above], axis=0)
        sources = [extended[m : m + rows] for m in range(2 * HALO + 1)]
        warped = []
        for p in range(frames // 2):
            taps = coefs[p * group : (p + 1) * group, :].astype(F32)
            for i in range(2):
                column = columns[2 * p + i]
                low = column == -2.0
                mid = column == -1.0
                total = None
                for k in range(TAPS):
                    start = (i * TAPS + k) * rows
                    chosen = jnp.where(
                        low, sources[k], jnp.where(mid, sources[k + 1], sources[k + 2])
                    )
                    term = taps[start : start + rows] * chosen
                    total = term if total is None else total + term
                warped.append(total)
        return warped

    grid4 = chips == 4
    across = (chip // 2) * 2 + 1 - lax.rem(chip, 2)
    along = lax.rem(chip + chips // 2, chips)

    def source(d):
        if grid4:
            there = (None, across, along, lax.rem(across + 2, 4))[d] if d else chip
        else:
            there = lax.rem(chip + chips - d, chips)
        return there * 2 + core

    def cross(d, j):
        block, target = me, lax.rem(chip + d, chips)
        if grid4:
            block = source(2) if d == 3 else me
            target = along if d == 2 else across
        return remote(
            gathered.at[block, j],
            gathered.at[block, j],
            ag_send.at[d, j],
            ag_recv.at[d, j],
            target * 2 + core,
        )

    def to_sibling(d, j):
        block = source(d)
        return remote(
            gathered.at[block, j],
            gathered.at[block, j],
            fw_send.at[d, j],
            fw_recv.at[d, j],
            sibling,
        )

    first = (2, 1) if grid4 else tuple(range(1, chips))
    order = (2, 1, 3) if grid4 else first

    def spread_chunk(j):
        for d in first:
            cross(d, j).start()
        to_sibling(0, j).start()

    def pass_chunk(j):
        for d in order:
            cross(d, j).wait_recv()
            if grid4 and d == 2:
                cross(3, j).start()
            to_sibling(d, j).start()

    partner_copies = [
        remote(measured_hbm, part_measured, pt_send.at[0], pt_recv.at[0], partner),
        remote(weight_hbm, part_weight, pt_send.at[1], pt_recv.at[1], partner),
        remote(red_hbm, part_red, pt_send.at[2], pt_recv.at[2], partner),
    ]
    local[1].wait()
    for t in range(count):
        tile_copy(t).start()
    outside = jnp.zeros((HALO, sector), F32)
    inner = [value[HALO : rows - HALO] for value in warp(outside, outside)]
    gathered[me, 0] = jnp.concatenate(inner, axis=0).astype(BF16)
    spread_chunk(0)
    exchange_wait(vol_out, vol_in, hv_send, hv_recv)
    outer = []
    for value in warp(vol_in[0], vol_in[1]):
        outer += [value[:HALO], value[rows - HALO :]]
    gathered[me, 1] = jnp.concatenate(outer, axis=0).astype(BF16)
    spread_chunk(1)
    for copy in partner_copies:
        copy.start()
    pass_chunk(0)
    pass_chunk(1)
    for j in range(2):
        for d in range(chips):
            to_sibling(d, j).wait_recv()

    def project(t, carry):
        tile_copy(t).wait()
        own_sector = jnp.int32(0)
        part_sector = jnp.int32(0)
        for s in range(blocks):
            own_sector = jnp.where(tile_index[me, s] == t, s, own_sector)
            part_sector = jnp.where(tile_index[partner, s] == t, s, part_sector)
        left = jnp.concatenate(
            [
                gathered[own_sector].reshape(stacked, sector),
                gathered[part_sector].reshape(stacked, sector),
            ],
            axis=0,
        )
        for n in range(VB):
            span = slice(n * view, (n + 1) * view)
            proj[:, span] += jnp.dot(left, tiles[t, :, span], preferred_element_type=F32)
        return carry

    proj[...] = jnp.zeros_like(proj)
    lax.fori_loop(0, count, project, 0)

    for copy in local[2:]:
        copy.wait()
    for copy in partner_copies:
        copy.wait_recv()

    inside = rows - 2 * HALO
    chunk = frames * inside

    def in_order(base):
        pieces = []
        for f in range(frames):
            a = base + f * inside
            b = base + chunk + f * 2 * HALO
            pieces += [proj[b : b + HALO, :], proj[a : a + inside, :], proj[b + HALO : b + 2 * HALO, :]]
        return jnp.concatenate(pieces, axis=0)

    wide = 256
    flip = lax.broadcasted_iota(jnp.int32, (wide, wide), 0) + lax.broadcasted_iota(
        jnp.int32, (wide, wide), 1
    )
    flip = jnp.where(flip == wide - 1, 1.0, 0.0).astype(BF16)
    swap = conj_view[0, 0] == 1
    residuals = [
        measured[...].astype(F32) - in_order(0),
        part_measured[...].astype(F32) - in_order(stacked),
    ]
    mirrors = []
    for value in residuals:
        high = value.astype(BF16)
        rest = (value - high.astype(F32)).astype(BF16)
        pieces = []
        for w in range(VB):
            for u in range(view // wide):
                start = w * view + view - (u + 1) * wide
                pieces.append(
                    jnp.dot(high[:, start : start + wide], flip, preferred_element_type=F32)
                    + jnp.dot(rest[:, start : start + wide], flip, preferred_element_type=F32)
                )
        each = view // wide
        head = jnp.concatenate(pieces[:each], axis=1)
        tail = jnp.concatenate(pieces[each:], axis=1)
        mirrors.append(
            jnp.concatenate(
                [jnp.where(swap, tail, head), jnp.where(swap, head, tail)], axis=1
            )
        )

    def combine(residual, mirrored, red, weight):
        red = jnp.broadcast_to(red[None, :], residual.shape)
        value = red * residual + (1.0 - red) * mirrored
        return (value * jnp.concatenate([weight] * frames, axis=0)).astype(BF16)

    weighted_ref[...] = combine(residuals[0], mirrors[1], redundancy[...], ray_weight[...])
    out_weighted = pltpu.make_async_copy(weighted_ref, weighted_hbm, out_sem.at[0])
    out_weighted.start()
    part_weighted[...] = combine(residuals[1], mirrors[0], part_red[...], part_weight[...])

    def partial(s):
        contract = (((1,), (1,)), ((), ()))
        own = lax.dot_general(
            weighted_ref[...], tiles[tile_index[me, s]], contract, preferred_element_type=F32
        )
        other = lax.dot_general(
            part_weighted[...], tiles[tile_index[partner, s]], contract, preferred_element_type=F32
        )
        return own + other

    ring = half // 2
    side = me // half
    place = lax.rem(me, half) // 2

    def sector_at(d, c):
        return side * half + lax.rem(place + d, ring) * 2 + c

    def sib_copy(d):
        return remote(sib_out.at[d], sib_in.at[d], sb_send.at[d], sb_recv.at[d], sibling)

    def far_copy(d):
        return remote(far_out.at[d], far_in.at[d], fr_send.at[d], fr_recv.at[d], sector_at(d, core))

    for d in range(1, ring):
        sib_out[d] = partial(sector_at(d, 1 - core)).astype(BF16)
        sib_copy(d).start()
    for d in range(1, ring):
        value = partial(sector_at(d, core))
        sib_copy(d).wait_recv()
        far_out[d] = (value + sib_in[d].astype(F32)).astype(BF16)
        far_copy(d).start()
    sib_out[0] = partial(sector_at(0, 1 - core)).astype(BF16)
    sib_copy(0).start()
    image = partial(me)
    for d in range(1, ring):
        far_copy(d).wait_recv()
        image = image + far_in[d].astype(F32)
    sib_copy(0).wait_recv()
    image = image + sib_in[0].astype(F32)

    spread = [jnp.zeros((rows, sector), F32) for _ in range(2 * HALO + 1)]
    for p in range(frames // 2):
        taps = coefs[p * group : (p + 1) * group, :].astype(F32)
        for i in range(2):
            f = 2 * p + i
            column = columns[f]
            slices = image[f * rows : (f + 1) * rows]
            for k in range(TAPS):
                start = (i * TAPS + k) * rows
                term = taps[start : start + rows] * slices
                for j in range(HALO + 1):
                    spread[k + j] = spread[k + j] + jnp.where(
                        column == float(j - HALO), term, 0.0
                    )
    empty = jnp.zeros((HALO, sector), F32)
    total = None
    for m in range(2 * HALO + 1):
        parts = [jnp.zeros((m, sector), F32)] if m else []
        parts.append(spread[m])
        if m < 2 * HALO:
            parts.append(jnp.zeros((2 * HALO - m, sector), F32))
        padded = jnp.concatenate(parts, axis=0)
        total = padded if total is None else total + padded
    adj_out[0] = total[:HALO]
    adj_out[1] = total[rows + HALO :]
    exchange(adj_out, adj_in, ha_send, ha_recv)
    for j in range(2):
        for d in order:
            cross(d, j).wait_send()
        for d in range(chips):
            to_sibling(d, j).wait_send()
    out_weighted.wait()
    for copy in partner_copies:
        copy.wait_send()
    for d in range(ring):
        sib_copy(d).wait_send()
    for d in range(1, ring):
        far_copy(d).wait_send()
    exchange_wait(adj_out, adj_in, ha_send, ha_recv)
    middle = jnp.zeros((rows - 2 * HALO, sector), F32)
    edges = jnp.concatenate([adj_in[0], middle, adj_in[1]], axis=0)
    adjoint = total[HALO : rows + HALO] + edges
    next_ref[...] = vol + voxel_weight[...] * adjoint
    out_next = pltpu.make_async_copy(next_ref, next_hbm, out_sem.at[1])
    out_next.start()
    out_next.wait()


def settle(next_in, weighted_in, next_out, weighted_out):
    next_out[...] = next_in[...]
    weighted_out[...] = weighted_in[...]


def body(
    volume,
    measured,
    tiles,
    tile_index,
    warp_coef,
    warp_offset,
    ray_weight,
    redundancy,
    conj_view,
    voxel_weight,
):
    frames, rows, rays = measured.shape
    sector = volume.shape[1]
    blocks = lax.axis_size("angle")
    slabs = lax.axis_size("frame")
    stacked = frames * rows
    ring = blocks // 4
    vmem = pl.BlockSpec(memory_space=pltpu.VMEM)
    hbm = pl.BlockSpec(memory_space=pl.ANY)
    smem = pl.BlockSpec(memory_space=pltpu.SMEM)
    dma = pltpu.SemaphoreType.DMA
    flops = 8 * stacked * blocks * sector * rays
    volume_next, weighted = pl.pallas_call(
        functools.partial(kernel, blocks, slabs, frames, rows),
        out_shape=(
            jax.ShapeDtypeStruct(volume.shape, F32),
            jax.ShapeDtypeStruct((stacked, rays), BF16),
        ),
        in_specs=[hbm, hbm, hbm, smem, hbm, vmem, hbm, hbm, smem, hbm],
        out_specs=(hbm, hbm),
        scratch_shapes=[
            pltpu.VMEM(volume.shape, F32),
            pltpu.VMEM((stacked, rays), BF16),
            pltpu.VMEM((frames * TAPS * rows, sector), BF16),
            pltpu.VMEM(ray_weight.shape, F32),
            pltpu.VMEM((rays,), F32),
            pltpu.VMEM(voxel_weight.shape, F32),
            pltpu.VMEM(volume.shape, F32),
            pltpu.VMEM((stacked, rays), BF16),
            pltpu.VMEM(tiles.shape, BF16),
            pltpu.VMEM((blocks, 2, stacked // 2, sector), BF16),
            pltpu.VMEM((2 * stacked, rays), F32),
            pltpu.VMEM((stacked, rays), BF16),
            pltpu.VMEM(ray_weight.shape, F32),
            pltpu.VMEM((rays,), F32),
            pltpu.VMEM((stacked, rays), BF16),
            pltpu.VMEM((2, HALO, sector), F32),
            pltpu.VMEM((2, HALO, sector), F32),
            pltpu.VMEM((2, HALO, sector), F32),
            pltpu.VMEM((2, HALO, sector), F32),
            pltpu.VMEM((ring, stacked, sector), BF16),
            pltpu.VMEM((ring, stacked, sector), BF16),
            pltpu.VMEM((ring, stacked, sector), BF16),
            pltpu.VMEM((ring, stacked, sector), BF16),
            dma((6,)),
            dma((2,)),
            dma((tiles.shape[0],)),
            dma((blocks // 2, 2)),
            dma((blocks // 2, 2)),
            dma((blocks // 2, 2)),
            dma((blocks // 2, 2)),
            dma((3,)),
            dma((3,)),
            dma((2,)),
            dma((2,)),
            dma((2,)),
            dma((2,)),
            dma((ring,)),
            dma((ring,)),
            dma((ring,)),
            dma((ring,)),
        ],
        cost_estimate=pl.CostEstimate(
            flops=flops, bytes_accessed=2 * tiles.size, transcendentals=0
        ),
        compiler_params=pltpu.CompilerParams(
            collective_id=0, has_side_effects=True, vmem_limit_bytes=62 * 1024 * 1024
        ),
    )(
        volume,
        measured.reshape(stacked, rays),
        tiles,
        tile_index,
        warp_coef.reshape(frames * TAPS * rows, sector),
        warp_offset,
        ray_weight,
        redundancy,
        conj_view,
        voxel_weight,
    )
    volume_next, weighted = pl.pallas_call(
        settle,
        out_shape=(
            jax.ShapeDtypeStruct(volume.shape, F32),
            jax.ShapeDtypeStruct((stacked, rays), BF16),
        ),
        in_specs=[vmem, vmem],
        out_specs=(vmem, vmem),
    )(volume_next, weighted)
    return volume_next, weighted.reshape(frames, rows, rays)


def solution(mesh):
    placed = (
        P("frame", "angle"),
        P(None, "frame", "angle"),
        P(),
        P(),
        P(None, None, "frame", "angle"),
        P(None, "frame"),
        P("frame", "angle"),
        P("angle"),
        P("angle", None),
        P("frame", "angle"),
    )
    return jax.shard_map(
        body,
        mesh=mesh,
        in_specs=placed,
        out_specs=(P("frame", "angle"), P(None, "frame", "angle")),
        check_vma=False,
    )
```

```python
import functools

import jax
import jax.numpy as jnp
from jax import lax
from jax.experimental import pallas as pl
from jax.experimental.pallas import tpu as pltpu
from jax.sharding import PartitionSpec as P

VB = 2
HALO = 2
TAPS = 3
MESH = pl.DeviceIdType.MESH
F32 = jnp.float32
BF16 = jnp.bfloat16


def kernel(
    blocks,
    slabs,
    frames,
    rows,
    volume_hbm,
    measured_hbm,
    tiles_hbm,
    tile_index,
    coefs_hbm,
    offsets,
    weight_hbm,
    red_hbm,
    conj_view,
    voxel_hbm,
    next_hbm,
    weighted_hbm,
    volume,
    measured,
    coefs,
    ray_weight,
    redundancy,
    voxel_weight,
    next_ref,
    weighted_ref,
    tiles,
    gathered,
    proj,
    part_measured,
    part_weight,
    part_red,
    part_weighted,
    vol_out,
    vol_in,
    adj_out,
    adj_in,
    sib_out,
    sib_in,
    far_out,
    far_in,
    in_sem,
    out_sem,
    tile_sem,
    ag_send,
    ag_recv,
    fw_send,
    fw_recv,
    pt_send,
    pt_recv,
    hv_send,
    hv_recv,
    ha_send,
    ha_recv,
    sb_send,
    sb_recv,
    fr_send,
    fr_recv,
):
    me = lax.axis_index("angle")
    slab = lax.axis_index("frame")
    half = blocks // 2
    chips = blocks // 2
    core = lax.rem(me, 2)
    chip = me // 2
    sibling = me + 1 - 2 * core
    partner = lax.rem(me + half, blocks)
    count = tiles.shape[0]
    stacked = frames * rows
    sector = volume.shape[1]
    rays = measured.shape[1]
    view = rays // VB
    has_low = slab > 0
    has_high = slab < slabs - 1

    def remote(src, dst, send, recv, angle, frame=slab):
        return pltpu.make_async_remote_copy(
            src_ref=src,
            dst_ref=dst,
            send_sem=send,
            recv_sem=recv,
            device_id=(angle, frame),
            device_id_type=MESH,
        )

    def tile_copy(t):
        return pltpu.make_async_copy(tiles_hbm.at[t], tiles.at[t], tile_sem.at[t])

    barrier = pltpu.get_barrier_semaphore()
    pl.semaphore_signal(barrier, inc=1, device_id=(sibling, slab), device_id_type=MESH)
    for d in range(1, chips):
        other = lax.rem(chip + d, chips) * 2 + core
        pl.semaphore_signal(barrier, inc=1, device_id=(other, slab), device_id_type=MESH)

    @pl.when(has_low)
    def _():
        pl.semaphore_signal(barrier, inc=1, device_id=(me, slab - 1), device_id_type=MESH)

    @pl.when(has_high)
    def _():
        pl.semaphore_signal(barrier, inc=1, device_id=(me, slab + 1), device_id_type=MESH)

    local = [
        pltpu.make_async_copy(src, dst, in_sem.at[n])
        for n, (src, dst) in enumerate(
            (
                (volume_hbm, volume),
                (coefs_hbm, coefs),
                (measured_hbm, measured),
                (weight_hbm, ray_weight),
                (red_hbm, redundancy),
                (voxel_hbm, voxel_weight),
            )
        )
    ]
    for copy in local:
        copy.start()
    local[0].wait()
    vol = volume[...]
    vol_out[0] = vol[:HALO]
    vol_out[1] = vol[rows - HALO :]

    peers = chips + has_low.astype(jnp.int32) + has_high.astype(jnp.int32)
    pl.semaphore_wait(barrier, peers)

    def halo(out, into, send, recv, side):
        return remote(
            out.at[side], into.at[1 - side], send.at[side], recv.at[1 - side], me, slab + 2 * side - 1
        )

    def exchange(out, into, send, recv):
        @pl.when(has_low)
        def _():
            halo(out, into, send, recv, 0).start()

        @pl.when(has_high)
        def _():
            halo(out, into, send, recv, 1).start()

    def exchange_wait(out, into, send, recv):
        @pl.when(has_low)
        def _():
            halo(out, into, send, recv, 0).wait_send()
            halo(out, into, send, recv, 1).wait_recv()

        @pl.when(has_high)
        def _():
            halo(out, into, send, recv, 1).wait_send()
            halo(out, into, send, recv, 0).wait_recv()

        @pl.when(slab == 0)
        def _():
            into[0] = jnp.zeros_like(into[0])

        @pl.when(slab == slabs - 1)
        def _():
            into[1] = jnp.zeros_like(into[1])

    exchange(vol_out, vol_in, hv_send, hv_recv)

    off = offsets[...].astype(F32)
    lane = lax.broadcasted_iota(jnp.int32, (rows, rows), 1)
    diagonal = lane == lax.broadcasted_iota(jnp.int32, (rows, rows), 0)

    def offset_column(f):
        spread = jnp.broadcast_to(off[f : f + 1, :], (rows, rows))
        return jnp.sum(jnp.where(diagonal, spread, 0.0), axis=1, keepdims=True)

    columns = [offset_column(f) for f in range(frames)]
    group = 2 * TAPS * rows

    def warp(below, above):
        extended = jnp.concatenate([below, vol, above], axis=0)
        sources = [extended[m : m + rows] for m in range(2 * HALO + 1)]
        warped = []
        for p in range(frames // 2):
            taps = coefs[p * group : (p + 1) * group, :].astype(F32)
            for i in range(2):
                column = columns[2 * p + i]
                low = column == -2.0
                mid = column == -1.0
                total = None
                for k in range(TAPS):
                    start = (i * TAPS + k) * rows
                    chosen = jnp.where(
                        low, sources[k], jnp.where(mid, sources[k + 1], sources[k + 2])
                    )
                    term = taps[start : start + rows] * chosen
                    total = term if total is None else total + term
                warped.append(total)
        return warped

    def source(d):
        return lax.rem(chip + chips - d, chips) * 2 + core

    def cross(d, j):
        return remote(
            gathered.at[me, j],
            gathered.at[me, j],
            ag_send.at[d, j],
            ag_recv.at[d, j],
            lax.rem(chip + d, chips) * 2 + core,
        )

    def to_sibling(d, j):
        block = source(d)
        return remote(
            gathered.at[block, j],
            gathered.at[block, j],
            fw_send.at[d, j],
            fw_recv.at[d, j],
            sibling,
        )

    order = range(1, chips)

    def spread_chunk(j):
        for d in order:
            cross(d, j).start()
        to_sibling(0, j).start()

    def pass_chunk(j):
        for d in order:
            cross(d, j).wait_recv()
            to_sibling(d, j).start()

    partner_copies = [
        remote(measured_hbm, part_measured, pt_send.at[0], pt_recv.at[0], partner),
        remote(weight_hbm, part_weight, pt_send.at[1], pt_recv.at[1], partner),
        remote(red_hbm, part_red, pt_send.at[2], pt_recv.at[2], partner),
    ]
    local[1].wait()
    for t in range(count):
        tile_copy(t).start()
    outside = jnp.zeros((HALO, sector), F32)
    inner = [value[HALO : rows - HALO] for value in warp(outside, outside)]
    gathered[me, 0] = jnp.concatenate(inner, axis=0).astype(BF16)
    spread_chunk(0)
    exchange_wait(vol_out, vol_in, hv_send, hv_recv)
    outer = []
    for value in warp(vol_in[0], vol_in[1]):
        outer += [value[:HALO], value[rows - HALO :]]
    gathered[me, 1] = jnp.concatenate(outer, axis=0).astype(BF16)
    spread_chunk(1)
    for copy in partner_copies:
        copy.start()
    pass_chunk(0)
    pass_chunk(1)
    for j in range(2):
        for d in range(chips):
            to_sibling(d, j).wait_recv()

    def project(t, carry):
        tile_copy(t).wait()
        own_sector = jnp.int32(0)
        part_sector = jnp.int32(0)
        for s in range(blocks):
            own_sector = jnp.where(tile_index[me, s] == t, s, own_sector)
            part_sector = jnp.where(tile_index[partner, s] == t, s, part_sector)
        left = jnp.concatenate(
            [
                gathered[own_sector].reshape(stacked, sector),
                gathered[part_sector].reshape(stacked, sector),
            ],
            axis=0,
        )
        for n in range(VB):
            span = slice(n * view, (n + 1) * view)
            proj[:, span] += jnp.dot(left, tiles[t, :, span], preferred_element_type=F32)
        return carry

    proj[...] = jnp.zeros_like(proj)
    lax.fori_loop(0, count, project, 0)

    for copy in local[2:]:
        copy.wait()
    for copy in partner_copies:
        copy.wait_recv()

    inside = rows - 2 * HALO
    chunk = frames * inside

    def in_order(base):
        pieces = []
        for f in range(frames):
            a = base + f * inside
            b = base + chunk + f * 2 * HALO
            pieces += [proj[b : b + HALO, :], proj[a : a + inside, :], proj[b + HALO : b + 2 * HALO, :]]
        return jnp.concatenate(pieces, axis=0)

    wide = 256
    flip = lax.broadcasted_iota(jnp.int32, (wide, wide), 0) + lax.broadcasted_iota(
        jnp.int32, (wide, wide), 1
    )
    flip = jnp.where(flip == wide - 1, 1.0, 0.0).astype(BF16)
    swap = conj_view[0, 0] == 1
    residuals = [
        measured[...].astype(F32) - in_order(0),
        part_measured[...].astype(F32) - in_order(stacked),
    ]
    mirrors = []
    for value in residuals:
        high = value.astype(BF16)
        rest = (value - high.astype(F32)).astype(BF16)
        pieces = []
        for w in range(VB):
            for u in range(view // wide):
                start = w * view + view - (u + 1) * wide
                pieces.append(
                    jnp.dot(high[:, start : start + wide], flip, preferred_element_type=F32)
                    + jnp.dot(rest[:, start : start + wide], flip, preferred_element_type=F32)
                )
        each = view // wide
        head = jnp.concatenate(pieces[:each], axis=1)
        tail = jnp.concatenate(pieces[each:], axis=1)
        mirrors.append(
            jnp.concatenate(
                [jnp.where(swap, tail, head), jnp.where(swap, head, tail)], axis=1
            )
        )

    def combine(residual, mirrored, red, weight):
        red = jnp.broadcast_to(red[None, :], residual.shape)
        value = red * residual + (1.0 - red) * mirrored
        return (value * jnp.concatenate([weight] * frames, axis=0)).astype(BF16)

    weighted_ref[...] = combine(residuals[0], mirrors[1], redundancy[...], ray_weight[...])
    out_weighted = pltpu.make_async_copy(weighted_ref, weighted_hbm, out_sem.at[0])
    out_weighted.start()
    part_weighted[...] = combine(residuals[1], mirrors[0], part_red[...], part_weight[...])

    def partial(s):
        contract = (((1,), (1,)), ((), ()))
        own = lax.dot_general(
            weighted_ref[...], tiles[tile_index[me, s]], contract, preferred_element_type=F32
        )
        other = lax.dot_general(
            part_weighted[...], tiles[tile_index[partner, s]], contract, preferred_element_type=F32
        )
        return own + other

    ring = half // 2
    side = me // half
    place = lax.rem(me, half) // 2

    def sector_at(d, c):
        return side * half + lax.rem(place + d, ring) * 2 + c

    def sib_copy(d):
        return remote(sib_out.at[d], sib_in.at[d], sb_send.at[d], sb_recv.at[d], sibling)

    def far_copy(d):
        return remote(far_out.at[d], far_in.at[d], fr_send.at[d], fr_recv.at[d], sector_at(d, core))

    for d in range(1, ring):
        sib_out[d] = partial(sector_at(d, 1 - core)).astype(BF16)
        sib_copy(d).start()
    for d in range(1, ring):
        value = partial(sector_at(d, core))
        sib_copy(d).wait_recv()
        far_out[d] = (value + sib_in[d].astype(F32)).astype(BF16)
        far_copy(d).start()
    sib_out[0] = partial(sector_at(0, 1 - core)).astype(BF16)
    sib_copy(0).start()
    image = partial(me)
    for d in range(1, ring):
        far_copy(d).wait_recv()
        image = image + far_in[d].astype(F32)
    sib_copy(0).wait_recv()
    image = image + sib_in[0].astype(F32)

    spread = [jnp.zeros((rows, sector), F32) for _ in range(2 * HALO + 1)]
    for p in range(frames // 2):
        taps = coefs[p * group : (p + 1) * group, :].astype(F32)
        for i in range(2):
            f = 2 * p + i
            column = columns[f]
            slices = image[f * rows : (f + 1) * rows]
            for k in range(TAPS):
                start = (i * TAPS + k) * rows
                term = taps[start : start + rows] * slices
                for j in range(HALO + 1):
                    spread[k + j] = spread[k + j] + jnp.where(
                        column == float(j - HALO), term, 0.0
                    )
    empty = jnp.zeros((HALO, sector), F32)
    total = None
    for m in range(2 * HALO + 1):
        parts = [jnp.zeros((m, sector), F32)] if m else []
        parts.append(spread[m])
        if m < 2 * HALO:
            parts.append(jnp.zeros((2 * HALO - m, sector), F32))
        padded = jnp.concatenate(parts, axis=0)
        total = padded if total is None else total + padded
    adj_out[0] = total[:HALO]
    adj_out[1] = total[rows + HALO :]
    exchange(adj_out, adj_in, ha_send, ha_recv)
    for j in range(2):
        for d in order:
            cross(d, j).wait_send()
        for d in range(chips):
            to_sibling(d, j).wait_send()
    out_weighted.wait()
    for copy in partner_copies:
        copy.wait_send()
    for d in range(ring):
        sib_copy(d).wait_send()
    for d in range(1, ring):
        far_copy(d).wait_send()
    exchange_wait(adj_out, adj_in, ha_send, ha_recv)
    middle = jnp.zeros((rows - 2 * HALO, sector), F32)
    edges = jnp.concatenate([adj_in[0], middle, adj_in[1]], axis=0)
    adjoint = total[HALO : rows + HALO] + edges
    next_ref[...] = vol + voxel_weight[...] * adjoint
    out_next = pltpu.make_async_copy(next_ref, next_hbm, out_sem.at[1])
    out_next.start()
    out_next.wait()


def settle(next_in, weighted_in, next_out, weighted_out):
    next_out[...] = next_in[...]
    weighted_out[...] = weighted_in[...]


def body(
    volume,
    measured,
    tiles,
    tile_index,
    warp_coef,
    warp_offset,
    ray_weight,
    redundancy,
    conj_view,
    voxel_weight,
):
    frames, rows, rays = measured.shape
    sector = volume.shape[1]
    blocks = lax.axis_size("angle")
    slabs = lax.axis_size("frame")
    stacked = frames * rows
    ring = blocks // 4
    vmem = pl.BlockSpec(memory_space=pltpu.VMEM)
    hbm = pl.BlockSpec(memory_space=pl.ANY)
    smem = pl.BlockSpec(memory_space=pltpu.SMEM)
    dma = pltpu.SemaphoreType.DMA
    flops = 8 * stacked * blocks * sector * rays
    volume_next, weighted = pl.pallas_call(
        functools.partial(kernel, blocks, slabs, frames, rows),
        out_shape=(
            jax.ShapeDtypeStruct(volume.shape, F32),
            jax.ShapeDtypeStruct((stacked, rays), BF16),
        ),
        in_specs=[hbm, hbm, hbm, smem, hbm, vmem, hbm, hbm, smem, hbm],
        out_specs=(hbm, hbm),
        scratch_shapes=[
            pltpu.VMEM(volume.shape, F32),
            pltpu.VMEM((stacked, rays), BF16),
            pltpu.VMEM((frames * TAPS * rows, sector), BF16),
            pltpu.VMEM(ray_weight.shape, F32),
            pltpu.VMEM((rays,), F32),
            pltpu.VMEM(voxel_weight.shape, F32),
            pltpu.VMEM(volume.shape, F32),
            pltpu.VMEM((stacked, rays), BF16),
            pltpu.VMEM(tiles.shape, BF16),
            pltpu.VMEM((blocks, 2, stacked // 2, sector), BF16),
            pltpu.VMEM((2 * stacked, rays), F32),
            pltpu.VMEM((stacked, rays), BF16),
            pltpu.VMEM(ray_weight.shape, F32),
            pltpu.VMEM((rays,), F32),
            pltpu.VMEM((stacked, rays), BF16),
            pltpu.VMEM((2, HALO, sector), F32),
            pltpu.VMEM((2, HALO, sector), F32),
            pltpu.VMEM((2, HALO, sector), F32),
            pltpu.VMEM((2, HALO, sector), F32),
            pltpu.VMEM((ring, stacked, sector), BF16),
            pltpu.VMEM((ring, stacked, sector), BF16),
            pltpu.VMEM((ring, stacked, sector), BF16),
            pltpu.VMEM((ring, stacked, sector), BF16),
            dma((6,)),
            dma((2,)),
            dma((tiles.shape[0],)),
            dma((blocks // 2, 2)),
            dma((blocks // 2, 2)),
            dma((blocks // 2, 2)),
            dma((blocks // 2, 2)),
            dma((3,)),
            dma((3,)),
            dma((2,)),
            dma((2,)),
            dma((2,)),
            dma((2,)),
            dma((ring,)),
            dma((ring,)),
            dma((ring,)),
            dma((ring,)),
        ],
        cost_estimate=pl.CostEstimate(
            flops=flops, bytes_accessed=2 * tiles.size, transcendentals=0
        ),
        compiler_params=pltpu.CompilerParams(
            collective_id=0, has_side_effects=True, vmem_limit_bytes=62 * 1024 * 1024
        ),
    )(
        volume,
        measured.reshape(stacked, rays),
        tiles,
        tile_index,
        warp_coef.reshape(frames * TAPS * rows, sector),
        warp_offset,
        ray_weight,
        redundancy,
        conj_view,
        voxel_weight,
    )
    volume_next, weighted = pl.pallas_call(
        settle,
        out_shape=(
            jax.ShapeDtypeStruct(volume.shape, F32),
            jax.ShapeDtypeStruct((stacked, rays), BF16),
        ),
        in_specs=[vmem, vmem],
        out_specs=(vmem, vmem),
    )(volume_next, weighted)
    return volume_next, weighted.reshape(frames, rows, rays)


def solution(mesh):
    placed = (
        P("frame", "angle"),
        P(None, "frame", "angle"),
        P(),
        P(),
        P(None, None, "frame", "angle"),
        P(None, "frame"),
        P("frame", "angle"),
        P("angle"),
        P("angle", None),
        P("frame", "angle"),
    )
    return jax.shard_map(
        body,
        mesh=mesh,
        in_specs=placed,
        out_specs=(P("frame", "angle"), P(None, "frame", "angle")),
        check_vma=False,
    )
```
